512 devices in a mesh: ctx: 64 (over y, z), head: 8 (over x, core).
Axes of the slice: x: 4, y: 8, z: 8, core: 2. Of those that a mesh axis runs over, the one named last changes fastest.
Arguments:
- query_in: bfloat16 [12288, 1024], P('ctx', 'head'), may hold values from -18 to 18
- key_in: bfloat16 [12288, 128], P(('ctx', 'head')), may hold values from -4 to 4
- value_in: bfloat16 [12288, 128], P(('ctx', 'head')), may hold values from -6 to 6
- grad_out: bfloat16 [12288, 1024], P('ctx', 'head'), may hold values from -6 to 6
- span_of: int32 [128], replicated, may hold values from 0 to 127, as said below
Outputs:
- attn_out: bfloat16 [12288, 1024], P(('ctx', 'head'))
- grad_query: bfloat16 [12288, 1024], P(('ctx', 'head'))
- grad_key: bfloat16 [12288, 128], P(('ctx', 'head'))
- grad_value: bfloat16 [12288, 128], P(('ctx', 'head'))
The draws below stay inside these ranges and needn't reach their ends.
Inputs may be any that keep to these rules, and one draw needn't show every extreme that they name: `span_of`: blocks 2c and 2c + 1 of 96 rows (those of context shard c) hold two spans whose numbers add up to 127; every span number occurs once.
All inputs are finite; a program needn't handle non-finite values.
Results may differ from the reference program's by a relative error of at most 0.018.
Values may be sent and summed in bfloat16 or wider, within the bound.
No kernel may reach another device: no remote copies, remote signals or barrier semaphores. Data moves between devices by JAX's collectives and lax.ppermute only.
A program may use at most 64 MiB of HBM per device.

```python
import math
import jax
import jax.numpy as jnp
from jax import lax

HD = 128
HEADS = 8
CH = 96
N_SPAN = 128
SEQ = 12288


def draw_key_in(key, part):
    key = jax.random.fold_in(key, 11)
    drawn = jnp.clip(jax.random.normal(key, (SEQ, HD), jnp.float32), -4.0, 4.0)
    return drawn.astype(jnp.bfloat16)


def draw_query_in(key, part):
    key = jax.random.fold_in(key, 12)
    drawn = jnp.clip(jax.random.normal(key, (SEQ, HEADS * HD), jnp.float32), -4.0, 4.0)
    return drawn.astype(jnp.bfloat16)


def draw_span_of(key, part):
    key = jax.random.fold_in(key, 5)
    first, second = jax.random.split(key)
    half_count = N_SPAN // 2
    paired = jax.random.permutation(first, half_count).astype(jnp.int32)
    flipped = jax.random.randint(second, (half_count,), 0, 2).astype(jnp.int32)
    leading = jnp.where(flipped == 1, paired, N_SPAN - 1 - paired)
    trailing = N_SPAN - 1 - leading
    return jnp.stack([leading, trailing], axis=1).reshape(N_SPAN).astype(jnp.int32)


def block_levels(key, dims, cuts, low, top_value):
    factor_of, own = 1.0, jax.random.fold_in(key, 6)
    for dim, blocks in cuts:
        heights = jnp.exp(jax.random.uniform(jax.random.fold_in(own, dim), (blocks,), jnp.float32, low / len(cuts), top_value / len(cuts)))
        factor_of = factor_of * jnp.repeat(heights, dims[dim] // blocks).reshape([-1 if axis == dim else 1 for axis in range(len(dims))])
    return factor_of


def scatter_about(rng, shape, spread, most, cuts=(), kind=jnp.bfloat16):
    array = spread * jax.random.normal(rng, shape, jnp.float32)
    if cuts:
        array = array * block_levels(rng, shape, cuts, -0.22, 0.18)
    return jnp.clip(array, -most, most).astype(kind)


def setup_inputs(seed: int = 0) -> dict:
    keys = jax.random.split(jax.random.key(seed), 6)
    return {
        "query_in": draw_query_in(jax.random.fold_in(keys[5], 71), 0),
        "key_in": draw_key_in(jax.random.fold_in(keys[5], 71), 0),
        "value_in": scatter_about(keys[2], (SEQ, HD), 1.0, 6.0, ((0, 512),)),
        "grad_out": scatter_about(keys[3], (SEQ, HEADS * HD), 1.0, 6.0, ((0, 64), (1, 8))),
        "span_of": draw_span_of(jax.random.fold_in(keys[5], 71), 0),
    }


def reference(query_in, key_in, value_in, grad_out, span_of):
    row_ids = jnp.arange(SEQ, dtype=jnp.int32)
    position = (span_of[row_ids // CH] * CH + row_ids % CH).astype(jnp.int32)
    ordering = jnp.argsort(position).astype(jnp.int32)
    scaling = 1.0 / math.sqrt(HD)
    key_rows = key_in[ordering]
    value_rows = value_in[ordering]
    queries = query_in[ordering].reshape(SEQ, HEADS, HD).transpose(1, 0, 2)
    douts = grad_out[ordering].reshape(SEQ, HEADS, HD).transpose(1, 0, 2)
    block_size = math.gcd(SEQ, 1024)
    block_count = SEQ // block_size
    key_ids = jnp.arange(SEQ, dtype=jnp.int32)

    def head_step(carried, inputs):
        head_q, head_do = inputs

        def block_step(state, number):
            grad_k, grad_v = state
            offset = number * block_size
            query_rows = lax.dynamic_slice_in_dim(head_q, offset, block_size, 0)
            dout_rows = lax.dynamic_slice_in_dim(head_do, offset, block_size, 0)
            query_pos = offset + jnp.arange(block_size, dtype=jnp.int32)
            scores = jnp.dot(query_rows, key_rows.T, preferred_element_type=jnp.float32) * scaling
            scores = jnp.where(key_ids[None, :] <= query_pos[:, None], scores, -jnp.inf)
            row_max = lax.optimization_barrier(jnp.max(scores, axis=1))
            log_total = row_max + jnp.log(lax.optimization_barrier(jnp.sum(jnp.exp(scores - row_max[:, None]), axis=1)))
            probs = jnp.exp(scores - log_total[:, None]).astype(jnp.bfloat16)
            out_rows = jnp.dot(probs, value_rows, preferred_element_type=jnp.float32).astype(jnp.bfloat16)
            dprobs = jnp.dot(dout_rows, value_rows.T, preferred_element_type=jnp.float32)
            widened = probs.astype(jnp.float32)
            delta_sum = lax.optimization_barrier(jnp.sum(widened * dprobs, axis=1))
            dscores = (widened * (dprobs - delta_sum[:, None]) * scaling).astype(jnp.bfloat16)
            dq_rows = jnp.dot(dscores, key_rows, preferred_element_type=jnp.float32).astype(jnp.bfloat16)
            grad_k = grad_k + jnp.dot(dscores.T, query_rows, preferred_element_type=jnp.float32)
            grad_v = grad_v + jnp.dot(probs.T, dout_rows, preferred_element_type=jnp.float32)
            return ((grad_k, grad_v), (out_rows, dq_rows))
        state, (out_blocks, dq_blocks) = lax.scan(block_step, carried, jnp.arange(block_count, dtype=jnp.int32))
        return (state, (out_blocks.reshape(SEQ, HD), dq_blocks.reshape(SEQ, HD)))
    initial = (jnp.zeros((SEQ, HD), jnp.float32), jnp.zeros((SEQ, HD), jnp.float32))
    (grad_k, grad_v), (out_heads, dq_heads) = lax.scan(head_step, initial, (queries, douts))
    attn_out = out_heads.transpose(1, 0, 2).reshape(SEQ, HEADS * HD)[position]
    grad_query = dq_heads.transpose(1, 0, 2).reshape(SEQ, HEADS * HD)[position]
    grad_key = grad_k.astype(jnp.bfloat16)[position]
    grad_value = grad_v.astype(jnp.bfloat16)[position]
    return (attn_out, grad_query, grad_key, grad_value)
```

```python
import functools
import math

import jax
import jax.numpy as jnp
from jax import lax
from jax.experimental import pallas as pl
from jax.experimental.pallas import tpu as pltpu
from jax.sharding import PartitionSpec as P

F32 = jnp.float32
BF16 = jnp.bfloat16
LOG2E = 1.4426950408889634
LOW = -1e30
NT = (((1,), (1,)), ((), ()))


def stage_rows(src_ref, q_s, d_s, heads, span, hd):
    for half in range(2):
        for h in range(heads):
            rows = src_ref[h, half * span : (half + 1) * span, :]
            q_s[half, h * span : (h + 1) * span, :] = rows[:, :hd]
            d_s[half, h * span : (h + 1) * span, :] = rows[:, hd:]


def stats_kernel(
    dims, rank_ref, tiles_ref, kpos_ref, qpos_ref, qd_ref, kv_ref,
    stat_ref, kvs_ref, kvt_ref, q_s, d_s, sort_s,
):
    heads, span, hd, chunks, kc, tk, rc = dims
    factor = LOG2E / math.sqrt(hd)

    def place(c, _):
        start = pl.multiple_of(rank_ref[c] * kc, kc)
        sort_s[pl.ds(start, kc), :] = kv_ref[c].astype(F32)
        return 0

    lax.fori_loop(0, chunks, place, 0)
    n_keys = chunks * kc
    for t in range(n_keys // tk):
        block = sort_s[t * tk : (t + 1) * tk, :]
        kvs_ref[t * tk : (t + 1) * tk, :] = block.astype(BF16)
        kvt_ref[:, t * tk : (t + 1) * tk] = block.T.astype(BF16)
    stage_rows(qd_ref, q_s, d_s, heads, span, hd)
    half_rows = heads * span
    for half in range(2):
        for r in range(half_rows // rc):
            cols = slice(r * rc, (r + 1) * rc)
            q = q_s[half, cols, :]
            d = d_s[half, cols, :]
            qpos = qpos_ref[half : half + 1, cols]

            def tile(t, carried):
                m, l, ds = carried
                keys = pl.ds(pl.multiple_of(t * tk, tk), tk)
                k = kvs_ref[keys, :hd]
                v = kvs_ref[keys, hd:]
                s = lax.dot_general(k, q, NT, preferred_element_type=F32) * factor
                s = jnp.where(kpos_ref[keys, :] <= qpos, s, LOW)
                dp = lax.dot_general(v, d, NT, preferred_element_type=F32)
                s = s.reshape(tk // 8, 8, rc)
                dp = dp.reshape(tk // 8, 8, rc)
                m_new = jnp.maximum(m, jnp.max(s, axis=0))
                keep = jnp.exp2(m - m_new)
                p = jnp.exp2(s - m_new[None])
                l = l * keep + jnp.sum(p, axis=0)
                ds = ds * keep + jnp.sum(p * dp, axis=0)
                return (m_new, l, ds)

            zero = jnp.zeros((8, rc), F32)
            m, l, ds = lax.fori_loop(
                0, tiles_ref[half], tile, (jnp.full((8, rc), LOW, F32), zero, zero)
            )
            top = jnp.max(m, axis=0, keepdims=True)
            w = jnp.exp2(m - top)
            l = jnp.maximum(jnp.sum(l * w, axis=0, keepdims=True), 1e-30)
            ds = jnp.sum(ds * w, axis=0, keepdims=True)
            out = slice(half * half_rows + r * rc, half * half_rows + (r + 1) * rc)
            stat_ref[0:1, out] = top + jnp.log2(l)
            stat_ref[1:2, out] = ds / l


def grad_kernel(
    dims, rank_ref, tiles_ref, kpos_ref, qpos_ref, stat_ref, qd_ref, kvs_ref, kvt_ref,
    rows_ref, dkv_ref, q_s, d_s, acc_s, o_s, dq_s, lse_s, delta_s,
):
    heads, span, hd, chunks, kc, tk, rc = dims
    scaling = 1.0 / math.sqrt(hd)
    factor = LOG2E * scaling
    half_rows = heads * span
    stage_rows(qd_ref, q_s, d_s, heads, span, hd)
    acc_s[...] = jnp.zeros_like(acc_s)
    o_s[...] = jnp.zeros_like(o_s)
    dq_s[...] = jnp.zeros_like(dq_s)
    parts = [stat_ref[h] for h in range(stat_ref.shape[0])]
    top = functools.reduce(jnp.maximum, [p[0:1] for p in parts])
    weights = [jnp.exp2(p[0:1] - top) for p in parts]
    total = functools.reduce(jnp.add, weights)
    weighted = functools.reduce(jnp.add, [w * p[1:2] for w, p in zip(weights, parts)])
    lse_s[...] = top + jnp.log2(total)
    delta_s[...] = weighted / total
    for half in range(2):
        for r in range(half_rows // rc):
            cols = slice(r * rc, (r + 1) * rc)
            out = slice(half * half_rows + r * rc, half * half_rows + (r + 1) * rc)
            qpos = qpos_ref[half : half + 1, cols]
            lse = lse_s[:, out]
            delta = delta_s[:, out]

            def tile(t, _):
                keys = pl.ds(pl.multiple_of(t * tk, tk), tk)
                q = q_s[half, cols, :]
                d = d_s[half, cols, :]
                k = kvs_ref[keys, :hd]
                v = kvs_ref[keys, hd:]
                s = lax.dot_general(k, q, NT, preferred_element_type=F32) * factor
                p = jnp.where(kpos_ref[keys, :] <= qpos, jnp.exp2(s - lse), 0.0)
                dp = lax.dot_general(v, d, NT, preferred_element_type=F32)
                pb = p.astype(BF16)
                g = (p * (dp - delta) * scaling).astype(BF16)
                acc_s[keys, :hd] += jnp.dot(g, q, preferred_element_type=F32)
                acc_s[keys, hd:] += jnp.dot(pb, d, preferred_element_type=F32)
                dq_s[:, out] += jnp.dot(kvt_ref[:hd, keys], g, preferred_element_type=F32)
                o_s[:, out] += jnp.dot(kvt_ref[hd:, keys], pb, preferred_element_type=F32)
                return 0

            lax.fori_loop(0, tiles_ref[half], tile, 0)

    def place(c, _):
        start = pl.multiple_of(rank_ref[c] * kc, kc)
        dkv_ref[c] = acc_s[pl.ds(start, kc), :].astype(BF16)
        return 0

    lax.fori_loop(0, chunks, place, 0)
    blocks = span // kc
    for which, src in enumerate((o_s, dq_s)):
        whole = src[...].T
        for half in range(2):
            for h in range(heads):
                for i in range(blocks):
                    first = half * half_rows + h * span + i * kc
                    at = which * heads * hd + h * hd
                    rows_ref[half * blocks + i, :, at : at + hd] = whole[
                        first : first + kc
                    ].astype(BF16)


def exchange(x, axis):
    return lax.all_to_all(x, axis, split_axis=0, concat_axis=0, tiled=True)


def local(query_in, key_in, value_in, grad_out, span_of):
    hd = key_in.shape[1]
    kc = key_in.shape[0]
    heads = lax.axis_size("head")
    shards = lax.axis_size("ctx")
    local_rows = query_in.shape[0]
    span = local_rows // 2
    n_keys = shards * kc
    tk = math.gcd(n_keys, 256)
    rc = math.gcd(heads * span, 256)
    dims = (heads, span, hd, shards, kc, tk, rc)
    blocks = span // kc
    ctx = lax.axis_index("ctx")
    head = lax.axis_index("head")

    spans = span_of.reshape(shards, 2)
    key_span = lax.dynamic_index_in_dim(spans, head // blocks, 1, keepdims=False)
    own = lax.dynamic_index_in_dim(spans, ctx, 0, keepdims=False)
    rank = jnp.sum((key_span[None, :] < key_span[:, None]).astype(jnp.int32), axis=1)
    slot = jnp.arange(shards, dtype=jnp.int32)
    ordered = jnp.sum(jnp.where(rank[None, :] == slot[:, None], key_span[None, :], 0), axis=1)
    kpos = (
        ordered[:, None] * span
        + (head % blocks) * kc
        + jnp.arange(kc, dtype=jnp.int32)[None, :]
    ).reshape(n_keys, 1)
    qpos = own[:, None] * span + jnp.tile(jnp.arange(span, dtype=jnp.int32), heads)[None, :]
    seen = jnp.sum((key_span[None, :] <= own[:, None]).astype(jnp.int32), axis=1) * kc
    tiles = (seen + tk - 1) // tk

    kv = jnp.concatenate([key_in, value_in], axis=1)
    qd = jnp.concatenate([query_in, grad_out], axis=1)
    kv_all = exchange(jnp.broadcast_to(kv[None], (shards, kc, 2 * hd)), "ctx")
    qd_all = exchange(jnp.broadcast_to(qd[None], (heads, local_rows, 2 * hd)), "head")

    smem = pl.BlockSpec(memory_space=pltpu.SMEM)
    vmem = pl.BlockSpec(memory_space=pltpu.VMEM)
    params = pltpu.CompilerParams(vmem_limit_bytes=48 * 1024 * 1024)
    half_rows = heads * span
    rows = 2 * half_rows
    stat, kvs, kvt = pl.pallas_call(
        functools.partial(stats_kernel, dims),
        out_shape=(
            jax.ShapeDtypeStruct((2, rows), F32),
            jax.ShapeDtypeStruct((n_keys, 2 * hd), BF16),
            jax.ShapeDtypeStruct((2 * hd, n_keys), BF16),
        ),
        in_specs=[smem, smem] + [vmem] * 4,
        out_specs=(vmem, vmem, vmem),
        scratch_shapes=[
            pltpu.VMEM((2, half_rows, hd), BF16),
            pltpu.VMEM((2, half_rows, hd), BF16),
            pltpu.VMEM((n_keys, 2 * hd), F32),
        ],
        compiler_params=params,
        name="attention_stats",
    )(rank, tiles, kpos, qpos, qd_all, kv_all)

    stat_all = exchange(jnp.broadcast_to(stat[None], (heads, 2, rows)), "head")

    row_parts, key_parts = pl.pallas_call(
        functools.partial(grad_kernel, dims),
        out_shape=(
            jax.ShapeDtypeStruct((heads, kc, 2 * heads * hd), BF16),
            jax.ShapeDtypeStruct((shards, kc, 2 * hd), BF16),
        ),
        in_specs=[smem, smem] + [vmem] * 6,
        out_specs=(vmem, vmem),
        scratch_shapes=[
            pltpu.VMEM((2, half_rows, hd), BF16),
            pltpu.VMEM((2, half_rows, hd), BF16),
            pltpu.VMEM((n_keys, 2 * hd), F32),
            pltpu.VMEM((hd, rows), F32),
            pltpu.VMEM((hd, rows), F32),
            pltpu.VMEM((1, rows), F32),
            pltpu.VMEM((1, rows), F32),
        ],
        compiler_params=params,
        name="attention_grads",
    )(rank, tiles, kpos, qpos, stat_all, qd_all, kvs, kvt)

    key_parts = exchange(key_parts, "ctx")
    row_parts = exchange(row_parts, "head")
    key_sum = jnp.sum(key_parts.astype(F32), axis=0).astype(BF16)
    row_sum = jnp.sum(row_parts.astype(F32), axis=0).astype(BF16)
    width = heads * hd
    return (row_sum[:, :width], row_sum[:, width:], key_sum[:, :hd], key_sum[:, hd:])


def solution(mesh):
    return jax.shard_map(
        local,
        mesh=mesh,
        in_specs=(
            P("ctx", "head"),
            P(("ctx", "head"), None),
            P(("ctx", "head"), None),
            P("ctx", "head"),
            P(),
        ),
        out_specs=(P(("ctx", "head"), None),) * 4,
        check_vma=False,
    )
```

```python
import functools
import math

import jax
import jax.numpy as jnp
from jax import lax
from jax.experimental import pallas as pl
from jax.experimental.pallas import tpu as pltpu
from jax.sharding import PartitionSpec as P

F32 = jnp.float32
BF16 = jnp.bfloat16
LOG2E = 1.4426950408889634
LOW = -1e30
NT = (((1,), (1,)), ((), ()))


def stage_rows(order_ref, sources, q_s, d_s, span, hd):
    number = 0
    for src_ref in sources:
        for piece in range(src_ref.shape[0]):
            at = pl.ds(pl.multiple_of(order_ref[number] * span, span), span)
            for half in range(2):
                rows = src_ref[piece, half * span : (half + 1) * span, :]
                q_s[half, at, :] = rows[:, :hd]
                d_s[half, at, :] = rows[:, hd:]
            number += 1


def stats_kernel(
    dims, rank_ref, tiles_ref, order_ref, kpos_ref, qpos_ref, near_ref, far_ref, kv_ref,
    stat_ref, kvs_ref, q_s, d_s, sort_s,
):
    heads, span, hd, chunks, kc, tk, rc = dims
    factor = LOG2E / math.sqrt(hd)

    def place(c, _):
        start = pl.multiple_of(rank_ref[c] * kc, kc)
        sort_s[pl.ds(start, kc), :] = kv_ref[c].astype(F32)
        return 0

    lax.fori_loop(0, chunks, place, 0)
    n_keys = chunks * kc
    for t in range(n_keys // tk):
        kvs_ref[t * tk : (t + 1) * tk, :] = sort_s[t * tk : (t + 1) * tk, :].astype(BF16)
    stage_rows(order_ref, (near_ref, far_ref), q_s, d_s, span, hd)
    half_rows = heads * span
    for half in range(2):
        for r in range(half_rows // rc):
            cols = slice(r * rc, (r + 1) * rc)
            q = q_s[half, cols, :]
            d = d_s[half, cols, :]
            qpos = qpos_ref[half : half + 1, cols]

            def tile(t, carried):
                m, l, ds = carried
                keys = pl.ds(pl.multiple_of(t * tk, tk), tk)
                k = kvs_ref[keys, :hd]
                v = kvs_ref[keys, hd:]
                s = lax.dot_general(k, q, NT, preferred_element_type=F32) * factor
                s = jnp.where(kpos_ref[keys, :] <= qpos, s, LOW)
                dp = lax.dot_general(v, d, NT, preferred_element_type=F32)
                s = s.reshape(tk // 8, 8, rc)
                dp = dp.reshape(tk // 8, 8, rc)
                m_new = jnp.maximum(m, jnp.max(s, axis=0))
                keep = jnp.exp2(m - m_new)
                p = jnp.exp2(s - m_new[None])
                l = l * keep + jnp.sum(p, axis=0)
                ds = ds * keep + jnp.sum(p * dp, axis=0)
                return (m_new, l, ds)

            zero = jnp.zeros((8, rc), F32)
            m, l, ds = lax.fori_loop(
                0, tiles_ref[half], tile, (jnp.full((8, rc), LOW, F32), zero, zero)
            )
            top = jnp.max(m, axis=0, keepdims=True)
            w = jnp.exp2(m - top)
            l = jnp.maximum(jnp.sum(l * w, axis=0, keepdims=True), 1e-30)
            ds = jnp.sum(ds * w, axis=0, keepdims=True)
            out = slice(half * half_rows + r * rc, half * half_rows + (r + 1) * rc)
            stat_ref[0:1, out] = top + jnp.log2(l)
            stat_ref[1:2, out] = ds / l


def grad_kernel(
    dims, rank_ref, tiles_ref, order_ref, kpos_ref, qpos_ref, stat_ref, near_ref, far_ref,
    kvs_ref, keep_ref, send_ref, dkv_ref,
    q_s, d_s, acc_s, o_s, dq_s, lse_s, delta_s, kvt_s, flat_s,
):
    heads, span, hd, chunks, kc, tk, rc = dims
    scaling = 1.0 / math.sqrt(hd)
    factor = LOG2E * scaling
    half_rows = heads * span
    stage_rows(order_ref, (near_ref, far_ref), q_s, d_s, span, hd)
    n_keys = chunks * kc
    for t in range(n_keys // tk):
        kvt_s[:, t * tk : (t + 1) * tk] = kvs_ref[t * tk : (t + 1) * tk, :].T
    acc_s[...] = jnp.zeros_like(acc_s)
    o_s[...] = jnp.zeros_like(o_s)
    dq_s[...] = jnp.zeros_like(dq_s)
    parts = [stat_ref[h] for h in range(stat_ref.shape[0])]
    top = functools.reduce(jnp.maximum, [p[0:1] for p in parts])
    weights = [jnp.exp2(p[0:1] - top) for p in parts]
    total = functools.reduce(jnp.add, weights)
    weighted = functools.reduce(jnp.add, [w * p[1:2] for w, p in zip(weights, parts)])
    lse_s[...] = top + jnp.log2(total)
    delta_s[...] = weighted / total
    for half in range(2):
        for r in range(half_rows // rc):
            cols = slice(r * rc, (r + 1) * rc)
            out = slice(half * half_rows + r * rc, half * half_rows + (r + 1) * rc)
            qpos = qpos_ref[half : half + 1, cols]
            lse = lse_s[:, out]
            delta = delta_s[:, out]

            def tile(t, _):
                keys = pl.ds(pl.multiple_of(t * tk, tk), tk)
                q = q_s[half, cols, :]
                d = d_s[half, cols, :]
                k = kvs_ref[keys, :hd]
                v = kvs_ref[keys, hd:]
                s = lax.dot_general(k, q, NT, preferred_element_type=F32) * factor
                p = jnp.where(kpos_ref[keys, :] <= qpos, jnp.exp2(s - lse), 0.0)
                dp = lax.dot_general(v, d, NT, preferred_element_type=F32)
                pb = p.astype(BF16)
                g = (p * (dp - delta) * scaling).astype(BF16)
                acc_s[keys, :hd] += jnp.dot(g, q, preferred_element_type=F32)
                acc_s[keys, hd:] += jnp.dot(pb, d, preferred_element_type=F32)
                dq_s[:, out] += jnp.dot(kvt_s[:hd, keys], g, preferred_element_type=F32)
                o_s[:, out] += jnp.dot(kvt_s[hd:, keys], pb, preferred_element_type=F32)
                return 0

            lax.fori_loop(0, tiles_ref[half], tile, 0)

    def place(c, _):
        start = pl.multiple_of(rank_ref[c] * kc, kc)
        dkv_ref[c] = acc_s[pl.ds(start, kc), :].astype(BF16)
        return 0

    lax.fori_loop(0, chunks, place, 0)
    blocks = span // kc
    per_core = heads // 2
    for which, src in enumerate((o_s, dq_s)):
        flat_s[...] = src[...].T
        for number in range(heads):
            target = order_ref[number]
            half, block = target // blocks, target % blocks
            out_ref = keep_ref if number < per_core else send_ref
            for h in range(heads):
                first = pl.multiple_of(half * half_rows + h * span + block * kc, kc)
                at = which * heads * hd + h * hd
                out_ref[number % per_core, :, at : at + hd] = flat_s[
                    pl.ds(first, kc), :
                ].astype(BF16)


def grouped(x, groups):
    return lax.all_to_all(
        x, ("ctx", "head"), split_axis=0, concat_axis=0, axis_index_groups=groups, tiled=True
    )


def line_groups(side, heads):
    first, second = [], []
    for head in range(heads):
        for fixed in range(side):
            along_z = [(fixed * side + moving) * heads + head for moving in range(side)]
            along_y = [(moving * side + fixed) * heads + head for moving in range(side)]
            first.append(along_y if head % 2 else along_z)
            second.append(along_z if head % 2 else along_y)
    return first, second


def flip_x(x, mesh_x, mask):
    pairs = [(2 * a + c, 2 * (a ^ mask) + c) for a in range(mesh_x) for c in range(2)]
    return lax.ppermute(x, "head", pairs)


def swap_cores(x, mesh_x):
    pairs = [(2 * a + c, 2 * a + 1 - c) for a in range(mesh_x) for c in range(2)]
    return lax.ppermute(x, "head", pairs)


def local(query_in, key_in, value_in, grad_out, span_of):
    hd = key_in.shape[1]
    kc = key_in.shape[0]
    heads = lax.axis_size("head")
    shards = lax.axis_size("ctx")
    local_rows = query_in.shape[0]
    span = local_rows // 2
    n_keys = shards * kc
    tk = math.gcd(n_keys, 256)
    rc = math.gcd(heads * span, 256)
    dims = (heads, span, hd, shards, kc, tk, rc)
    blocks = span // kc
    ctx = lax.axis_index("ctx")
    head = lax.axis_index("head")

    mesh_x = heads // 2
    at_x, core = head // 2, head % 2
    masks = [2 ** (bit + 1) - 1 for bit in range(mesh_x.bit_length() - 1)]
    offsets = [0]
    for mask in masks:
        offsets = offsets + [mask ^ offset for offset in offsets]
    origin = jnp.bitwise_xor(at_x, jnp.array(offsets, jnp.int32)) * 2
    order = jnp.concatenate([origin + core, origin + 1 - core]).astype(jnp.int32)
    side = math.isqrt(shards)
    first, second = line_groups(side, heads)

    spans = span_of.reshape(shards, 2)
    key_span = lax.dynamic_index_in_dim(spans, head // blocks, 1, keepdims=False)
    own = lax.dynamic_index_in_dim(spans, ctx, 0, keepdims=False)
    rank = jnp.sum((key_span[None, :] < key_span[:, None]).astype(jnp.int32), axis=1)
    place = jnp.arange(shards, dtype=jnp.int32)
    crossed = rank.reshape(side, side).T.reshape(shards)
    slots = jnp.where(core == 0, rank, crossed)
    ordered = jnp.sum(jnp.where(rank[None, :] == place[:, None], key_span[None, :], 0), axis=1)
    kpos = (
        ordered[:, None] * span
        + (head % blocks) * kc
        + jnp.arange(kc, dtype=jnp.int32)[None, :]
    ).reshape(n_keys, 1)
    qpos = own[:, None] * span + jnp.tile(jnp.arange(span, dtype=jnp.int32), heads)[None, :]
    seen = jnp.sum((key_span[None, :] <= own[:, None]).astype(jnp.int32), axis=1) * kc
    tiles = (seen + tk - 1) // tk

    kv = jnp.concatenate([key_in, value_in], axis=1)
    qd = jnp.concatenate([query_in, grad_out], axis=1)
    kv_line = grouped(jnp.broadcast_to(kv[None], (side, kc, 2 * hd)), first)
    kv_all = grouped(jnp.broadcast_to(kv_line[None], (side, side, kc, 2 * hd)), second)
    kv_all = kv_all.reshape(shards, kc, 2 * hd)
    near = qd[None]
    for mask in masks:
        near = jnp.concatenate([near, flip_x(near, mesh_x, mask)])
    far = swap_cores(near, mesh_x)

    smem = pl.BlockSpec(memory_space=pltpu.SMEM)
    vmem = pl.BlockSpec(memory_space=pltpu.VMEM)
    params = pltpu.CompilerParams(vmem_limit_bytes=48 * 1024 * 1024)
    half_rows = heads * span
    rows = 2 * half_rows
    stat, kvs = pl.pallas_call(
        functools.partial(stats_kernel, dims),
        out_shape=(
            jax.ShapeDtypeStruct((2, rows), F32),
            jax.ShapeDtypeStruct((n_keys, 2 * hd), BF16),
        ),
        in_specs=[smem] * 3 + [vmem] * 5,
        out_specs=(vmem, vmem),
        scratch_shapes=[
            pltpu.VMEM((2, half_rows, hd), BF16),
            pltpu.VMEM((2, half_rows, hd), BF16),
            pltpu.VMEM((n_keys, 2 * hd), F32),
        ],
        compiler_params=params,
        name="attention_stats",
    )(slots, tiles, order, kpos, qpos, near, far, kv_all)

    stat_all = lax.all_to_all(
        jnp.broadcast_to(stat[None], (heads, 2, rows)), "head", 0, 0, tiled=True
    )

    keep, send, key_parts = pl.pallas_call(
        functools.partial(grad_kernel, dims),
        out_shape=(
            jax.ShapeDtypeStruct((mesh_x, kc, 2 * heads * hd), BF16),
            jax.ShapeDtypeStruct((mesh_x, kc, 2 * heads * hd), BF16),
            jax.ShapeDtypeStruct((shards, kc, 2 * hd), BF16),
        ),
        in_specs=[smem] * 3 + [vmem] * 6,
        out_specs=(vmem, vmem, vmem),
        scratch_shapes=[
            pltpu.VMEM((2, half_rows, hd), BF16),
            pltpu.VMEM((2, half_rows, hd), BF16),
            pltpu.VMEM((n_keys, 2 * hd), F32),
            pltpu.VMEM((hd, rows), F32),
            pltpu.VMEM((hd, rows), F32),
            pltpu.VMEM((1, rows), F32),
            pltpu.VMEM((1, rows), F32),
            pltpu.VMEM((2 * hd, n_keys), BF16),
            pltpu.VMEM((rows, hd), F32),
        ],
        compiler_params=params,
        name="attention_grads",
    )(slots, tiles, order, kpos, qpos, stat_all, near, far, kvs)

    key_line = grouped(key_parts.reshape(side, side, kc, 2 * hd), second)
    key_line = jnp.sum(key_line.astype(F32), axis=0).astype(BF16)
    key_sum = jnp.sum(grouped(key_line, first).astype(F32), axis=0).astype(BF16)

    row_sum = keep.astype(F32) + swap_cores(send, mesh_x).astype(F32)
    for mask in reversed(masks):
        half = row_sum.shape[0] // 2
        moved = flip_x(row_sum[half:].astype(BF16), mesh_x, mask)
        row_sum = row_sum[:half] + moved.astype(F32)
    row_sum = row_sum[0].astype(BF16)
    width = heads * hd
    return (row_sum[:, :width], row_sum[:, width:], key_sum[:, :hd], key_sum[:, hd:])


def solution(mesh):
    return jax.shard_map(
        local,
        mesh=mesh,
        in_specs=(
            P("ctx", "head"),
            P(("ctx", "head"), None),
            P(("ctx", "head"), None),
            P("ctx", "head"),
            P(),
        ),
        out_specs=(P(("ctx", "head"), None),) * 4,
        check_vma=False,
    )
```

```python
import functools
import math

import jax
import jax.numpy as jnp
from jax import lax
from jax.experimental import pallas as pl
from jax.experimental.pallas import tpu as pltpu
from jax.sharding import PartitionSpec as P

F32 = jnp.float32
BF16 = jnp.bfloat16
LOG2E = 1.4426950408889634
LOW = -1e30
NT = (((1,), (1,)), ((), ()))


def stage_rows(order_ref, sources, q_ref, d_ref, span, hd):
    number = 0
    for src_ref in sources:
        for piece in range(src_ref.shape[0]):
            at = pl.ds(pl.multiple_of(order_ref[number] * span, span), span)
            for half in range(2):
                rows = src_ref[piece, half * span : (half + 1) * span, :]
                q_ref[half, at, :] = rows[:, :hd]
                d_ref[half, at, :] = rows[:, hd:]
            number += 1


def columns(half, half_rows, r, rc):
    first = half * half_rows + r * rc
    return slice(first, first + rc)


def stats_kernel(
    dims, slots_ref, tiles_ref, order_ref, kpos_ref, qpos_ref, near_ref, far_ref, kv_ref,
    stat_ref, kvs_ref, q_ref, d_ref, p_ref, s_s, sort_s,
):
    heads, span, hd, chunks, kc, tk, rc = dims
    factor = LOG2E / math.sqrt(hd)
    half_rows = heads * span
    parts = range(half_rows // rc)

    def place(c, _):
        start = pl.multiple_of(slots_ref[c] * kc, kc)
        sort_s[pl.ds(start, kc), :] = kv_ref[c].astype(F32)
        return 0

    lax.fori_loop(0, chunks, place, 0, unroll=4)
    for t in range(chunks * kc // tk):
        kvs_ref[t * tk : (t + 1) * tk, :] = sort_s[t * tk : (t + 1) * tk, :].astype(BF16)
    stage_rows(order_ref, (near_ref, far_ref), q_ref, d_ref, span, hd)

    for half in range(2):

        def score(masked, t, tops):
            keys = pl.ds(pl.multiple_of(t * tk, tk), tk)
            k = kvs_ref[keys, :hd]
            new = []
            for r in parts:
                cols = slice(r * rc, (r + 1) * rc)
                s = lax.dot_general(k, q_ref[half, cols, :], NT, preferred_element_type=F32)
                s = s * factor
                if masked:
                    s = jnp.where(kpos_ref[keys, :] <= qpos_ref[half : half + 1, cols], s, LOW)
                s_s[keys, cols] = s
                new.append(jnp.maximum(tops[r], jnp.max(s.reshape(tk // 8, 8, rc), axis=0)))
            return tuple(new)

        full, count = tiles_ref[2 * half], tiles_ref[2 * half + 1]
        tops = tuple(jnp.full((8, rc), LOW, F32) for _ in parts)
        tops = lax.fori_loop(0, full, functools.partial(score, False), tops)
        tops = lax.fori_loop(full, count, functools.partial(score, True), tops)
        tops = [jnp.max(top, axis=0, keepdims=True) for top in tops]

        def weigh(t, carried):
            keys = pl.ds(pl.multiple_of(t * tk, tk), tk)
            v = kvs_ref[keys, hd:]
            new = []
            for r in parts:
                cols = slice(r * rc, (r + 1) * rc)
                l, ds = carried[r]
                dp = lax.dot_general(v, d_ref[half, cols, :], NT, preferred_element_type=F32)
                p = jnp.exp2(s_s[keys, cols] - tops[r])
                p_ref[keys, columns(half, half_rows, r, rc)] = p.astype(BF16)
                l = l + jnp.sum(p.reshape(tk // 8, 8, rc), axis=0)
                ds = ds + jnp.sum((p * dp).reshape(tk // 8, 8, rc), axis=0)
                new.append((l, ds))
            return tuple(new)

        zero = jnp.zeros((8, rc), F32)
        sums = lax.fori_loop(0, count, weigh, tuple((zero, zero) for _ in parts))
        for r in parts:
            l = jnp.maximum(jnp.sum(sums[r][0], axis=0, keepdims=True), 1e-30)
            ds = jnp.sum(sums[r][1], axis=0, keepdims=True)
            out = columns(half, half_rows, r, rc)
            stat_ref[0:1, out] = tops[r] + jnp.log2(l)
            stat_ref[1:2, out] = ds / l
            stat_ref[2:3, out] = tops[r]


def grad_kernel(
    dims, slots_ref, tiles_ref, order_ref, stat_ref, all_ref, q_ref, d_ref, kvs_ref, p_ref,
    keep_ref, send_ref, dkv_ref, acc_s, o_s, dq_s, kvt_s, w_s, delta_s, flat_s,
):
    heads, span, hd, chunks, kc, tk, rc = dims
    scaling = 1.0 / math.sqrt(hd)
    half_rows = heads * span
    parts = range(half_rows // rc)
    for t in range(chunks * kc // tk):
        kvt_s[:, t * tk : (t + 1) * tk] = kvs_ref[t * tk : (t + 1) * tk, :].T
    acc_s[...] = jnp.zeros_like(acc_s)
    o_s[...] = jnp.zeros_like(o_s)
    dq_s[...] = jnp.zeros_like(dq_s)
    every = [all_ref[h] for h in range(all_ref.shape[0])]
    top = functools.reduce(jnp.maximum, [e[0:1] for e in every])
    weights = [jnp.exp2(e[0:1] - top) for e in every]
    total = functools.reduce(jnp.add, weights)
    weighted = functools.reduce(jnp.add, [w * e[1:2] for w, e in zip(weights, every)])
    w_s[...] = jnp.exp2(stat_ref[2:3, :] - top - jnp.log2(total))
    delta_s[...] = weighted / total
    for half in range(2):

        def tile(t, _):
            keys = pl.ds(pl.multiple_of(t * tk, tk), tk)
            v = kvs_ref[keys, hd:]
            dk = dv = None
            for r in parts:
                cols = slice(r * rc, (r + 1) * rc)
                out = columns(half, half_rows, r, rc)
                q, d = q_ref[half, cols, :], d_ref[half, cols, :]
                p = p_ref[keys, out].astype(F32) * w_s[:, out]
                dp = lax.dot_general(v, d, NT, preferred_element_type=F32)
                pb = p.astype(BF16)
                g = (p * (dp - delta_s[:, out])).astype(BF16)
                one = jnp.dot(g, q, preferred_element_type=F32)
                two = jnp.dot(pb, d, preferred_element_type=F32)
                dk, dv = (one, two) if dk is None else (dk + one, dv + two)
                dq_s[:, out] += jnp.dot(kvt_s[:hd, keys], g, preferred_element_type=F32)
                o_s[:, out] += jnp.dot(kvt_s[hd:, keys], pb, preferred_element_type=F32)
            acc_s[keys, :hd] += dk
            acc_s[keys, hd:] += dv
            return 0

        lax.fori_loop(0, tiles_ref[2 * half + 1], tile, 0)

    def place(c, _):
        start = pl.multiple_of(slots_ref[c] * kc, kc)
        rows = acc_s[pl.ds(start, kc), :]
        dkv_ref[c, :, :hd] = (rows[:, :hd] * scaling).astype(BF16)
        dkv_ref[c, :, hd:] = rows[:, hd:].astype(BF16)
        return 0

    lax.fori_loop(0, chunks, place, 0, unroll=4)
    blocks = span // kc
    per_core = heads // 2
    for which, (src, scale) in enumerate(((o_s, 1.0), (dq_s, scaling))):
        flat_s[...] = (src[...] * scale).T
        for number in range(heads):
            target = order_ref[number]
            half, block = target // blocks, target % blocks
            out_ref = keep_ref if number < per_core else send_ref
            for h in range(heads):
                first = pl.multiple_of(half * half_rows + h * span + block * kc, kc)
                at = which * heads * hd + h * hd
                out_ref[number % per_core, :, at : at + hd] = flat_s[
                    pl.ds(first, kc), :
                ].astype(BF16)


def run_stats(dims, slots, tiles, order, kpos, qpos, near, far, kv_all):
    heads, span, hd, chunks, kc, _, _ = dims
    half_rows, n_keys = heads * span, chunks * kc
    smem = pl.BlockSpec(memory_space=pltpu.SMEM)
    vmem = pl.BlockSpec(memory_space=pltpu.VMEM)
    return pl.pallas_call(
        functools.partial(stats_kernel, dims),
        out_shape=(
            jax.ShapeDtypeStruct((3, 2 * half_rows), F32),
            jax.ShapeDtypeStruct((n_keys, 2 * hd), BF16),
            jax.ShapeDtypeStruct((2, half_rows, hd), BF16),
            jax.ShapeDtypeStruct((2, half_rows, hd), BF16),
            jax.ShapeDtypeStruct((n_keys, 2 * half_rows), BF16),
        ),
        in_specs=[smem] * 3 + [vmem] * 5,
        out_specs=(vmem,) * 5,
        scratch_shapes=[
            pltpu.VMEM((n_keys, half_rows), F32),
            pltpu.VMEM((n_keys, 2 * hd), F32),
        ],
        compiler_params=pltpu.CompilerParams(vmem_limit_bytes=32 * 1024 * 1024),
        name="attention_stats",
    )(slots, tiles, order, kpos, qpos, near, far, kv_all)


def run_grads(dims, slots, tiles, order, stat, stat_all, q, d, kvs, probs):
    heads, span, hd, chunks, kc, _, _ = dims
    rows, n_keys = 2 * heads * span, chunks * kc
    smem = pl.BlockSpec(memory_space=pltpu.SMEM)
    vmem = pl.BlockSpec(memory_space=pltpu.VMEM)
    return pl.pallas_call(
        functools.partial(grad_kernel, dims),
        out_shape=(
            jax.ShapeDtypeStruct((heads // 2, kc, 2 * heads * hd), BF16),
            jax.ShapeDtypeStruct((heads // 2, kc, 2 * heads * hd), BF16),
            jax.ShapeDtypeStruct((chunks, kc, 2 * hd), BF16),
        ),
        in_specs=[smem] * 3 + [vmem] * 6,
        out_specs=(vmem,) * 3,
        scratch_shapes=[
            pltpu.VMEM((n_keys, 2 * hd), F32),
            pltpu.VMEM((hd, rows), F32),
            pltpu.VMEM((hd, rows), F32),
            pltpu.VMEM((2 * hd, n_keys), BF16),
            pltpu.VMEM((1, rows), F32),
            pltpu.VMEM((1, rows), F32),
            pltpu.VMEM((rows, hd), F32),
        ],
        compiler_params=pltpu.CompilerParams(vmem_limit_bytes=32 * 1024 * 1024),
        name="attention_grads",
    )(slots, tiles, order, stat, stat_all, q, d, kvs, probs)


def grouped(x, groups):
    return lax.all_to_all(
        x, ("ctx", "head"), split_axis=0, concat_axis=0, axis_index_groups=groups, tiled=True
    )


def line_groups(side, heads):
    first, second = [], []
    for head in range(heads):
        for fixed in range(side):
            along_z = [(fixed * side + moving) * heads + head for moving in range(side)]
            along_y = [(moving * side + fixed) * heads + head for moving in range(side)]
            first.append(along_y if head % 2 else along_z)
            second.append(along_z if head % 2 else along_y)
    return first, second


def flip_x(x, mesh_x, mask):
    pairs = [(2 * a + c, 2 * (a ^ mask) + c) for a in range(mesh_x) for c in range(2)]
    return lax.ppermute(x, "head", pairs)


def swap_cores(x, mesh_x):
    pairs = [(2 * a + c, 2 * a + 1 - c) for a in range(mesh_x) for c in range(2)]
    return lax.ppermute(x, "head", pairs)


def local(query_in, key_in, value_in, grad_out, span_of):
    hd = key_in.shape[1]
    kc = key_in.shape[0]
    heads = lax.axis_size("head")
    shards = lax.axis_size("ctx")
    local_rows = query_in.shape[0]
    span = local_rows // 2
    n_keys = shards * kc
    tk = math.gcd(n_keys, 256)
    rc = heads * span
    dims = (heads, span, hd, shards, kc, tk, rc)
    blocks = span // kc
    ctx = lax.axis_index("ctx")
    head = lax.axis_index("head")

    mesh_x = heads // 2
    at_x, core = head // 2, head % 2
    masks = [2 ** (bit + 1) - 1 for bit in range(mesh_x.bit_length() - 1)]
    offsets = [0]
    for mask in masks:
        offsets = offsets + [mask ^ offset for offset in offsets]
    origin = jnp.bitwise_xor(at_x, jnp.array(offsets, jnp.int32)) * 2
    order = jnp.concatenate([origin + core, origin + 1 - core]).astype(jnp.int32)
    side = math.isqrt(shards)
    first, second = line_groups(side, heads)

    spans = span_of.reshape(shards, 2)
    key_span = lax.dynamic_index_in_dim(spans, head // blocks, 1, keepdims=False)
    own = lax.dynamic_index_in_dim(spans, ctx, 0, keepdims=False)
    rank = jnp.sum((key_span[None, :] < key_span[:, None]).astype(jnp.int32), axis=1)
    place = jnp.arange(shards, dtype=jnp.int32)
    crossed = rank.reshape(side, side).T.reshape(shards)
    slots = jnp.where(core == 0, rank, crossed)
    ordered = jnp.sum(jnp.where(rank[None, :] == place[:, None], key_span[None, :], 0), axis=1)
    kpos = (
        ordered[:, None] * span
        + (head % blocks) * kc
        + jnp.arange(kc, dtype=jnp.int32)[None, :]
    ).reshape(n_keys, 1)
    qpos = own[:, None] * span + jnp.tile(jnp.arange(span, dtype=jnp.int32), heads)[None, :]
    before = jnp.sum((key_span[None, :] < own[:, None]).astype(jnp.int32), axis=1) * kc
    seen = jnp.sum((key_span[None, :] <= own[:, None]).astype(jnp.int32), axis=1) * kc
    tiles = jnp.stack([before // tk, (seen + tk - 1) // tk], axis=1).reshape(4)

    kv = jnp.concatenate([key_in, value_in], axis=1)
    qd = jnp.concatenate([query_in, grad_out], axis=1)
    near = qd[None]
    near = jnp.concatenate([near, flip_x(near, mesh_x, masks[0])])
    kv_line = grouped(jnp.broadcast_to(kv[None], (side, kc, 2 * hd)), first)
    kv_line, near = lax.optimization_barrier((kv_line, near))
    kv_all = grouped(jnp.broadcast_to(kv_line[None], (side, side, kc, 2 * hd)), second)
    kv_all = kv_all.reshape(shards, kc, 2 * hd)
    for mask in masks[1:]:
        near = jnp.concatenate([near, flip_x(near, mesh_x, mask)])
    far = swap_cores(near, mesh_x)

    stat, kvs, q, d, probs = run_stats(dims, slots, tiles, order, kpos, qpos, near, far, kv_all)
    rows = 2 * heads * span
    stat_all = lax.all_to_all(
        jnp.broadcast_to(stat[None, :2], (heads, 2, rows)), "head", 0, 0, tiled=True
    )
    keep, send, key_parts = run_grads(
        dims, slots, tiles, order, stat, stat_all, q, d, kvs, probs
    )

    key_line = grouped(key_parts.reshape(side, side, kc, 2 * hd), second)
    key_line = jnp.sum(key_line.astype(F32), axis=0).astype(BF16)

    row_sum = keep.astype(F32) + swap_cores(send, mesh_x).astype(F32)
    for mask in reversed(masks):
        if mask == masks[0]:
            key_line, row_sum = lax.optimization_barrier((key_line, row_sum))
            key_sum = jnp.sum(grouped(key_line, first).astype(F32), axis=0).astype(BF16)
        half = row_sum.shape[0] // 2
        moved = flip_x(row_sum[half:].astype(BF16), mesh_x, mask)
        row_sum = row_sum[:half] + moved.astype(F32)
    row_sum = row_sum[0].astype(BF16)
    width = heads * hd
    return (row_sum[:, :width], row_sum[:, width:], key_sum[:, :hd], key_sum[:, hd:])


def solution(mesh):
    return jax.shard_map(
        local,
        mesh=mesh,
        in_specs=(
            P("ctx", "head"),
            P(("ctx", "head"), None),
            P(("ctx", "head"), None),
            P("ctx", "head"),
            P(),
        ),
        out_specs=(P(("ctx", "head"), None),) * 4,
        check_vma=False,
    )
```

```python
import functools
import math

import jax
import jax.numpy as jnp
from jax import lax
from jax.experimental import pallas as pl
from jax.experimental.pallas import tpu as pltpu
from jax.sharding import PartitionSpec as P

F32 = jnp.float32
BF16 = jnp.bfloat16
LOG2E = 1.4426950408889634
LOW = -1e30
NT = (((1,), (1,)), ((), ()))


def stage_rows(order_ref, sources, q_ref, d_ref, span, hd):
    for number, src_ref in enumerate(sources):
        at = pl.ds(pl.multiple_of(order_ref[number] * span, span), span)
        for half in range(2):
            rows = src_ref[half * span : (half + 1) * span, :]
            q_ref[half, at, :] = rows[:, :hd]
            d_ref[half, at, :] = rows[:, hd:]


def tile_copies(pairs, sems, half, t, tk):
    at = (half, pl.ds(pl.multiple_of(t * tk, tk), tk))
    return [
        pltpu.make_async_copy(src.at[at], dst.at[at], sems.at[which, half, t])
        for which, (src, dst) in enumerate(pairs)
    ]


def start_all(tiles_ref, pairs, sems, tk):
    for half in range(2):

        def step(t, _):
            for copy in tile_copies(pairs, sems, half, t, tk):
                copy.start()
            return 0

        lax.fori_loop(0, tiles_ref[2 * half + 1], step, 0)


def wait_all(tiles_ref, pairs, sems, tk):
    for half in range(2):

        def step(t, _):
            for copy in tile_copies(pairs, sems, half, t, tk):
                copy.wait()
            return 0

        lax.fori_loop(0, tiles_ref[2 * half + 1], step, 0)


def columns(half, half_rows, r, rc):
    first = half * half_rows + r * rc
    return slice(first, first + rc)


def stats_kernel(
    dims, slots_ref, tiles_ref, order_ref, kpos_ref, qpos_ref, kv_ref, *refs
):
    heads, span, hd, chunks, kc, tk, rc = dims
    row_refs = refs[:heads]
    stat_ref, kvs_ref, q_ref, d_ref, probs_ref, s_s, sort_s, p_s, sems = refs[heads:]
    pairs = ((p_s, probs_ref),)
    factor = LOG2E / math.sqrt(hd)
    half_rows = heads * span
    parts = range(half_rows // rc)

    def place(c, _):
        start = pl.multiple_of(slots_ref[c] * kc, kc)
        sort_s[pl.ds(start, kc), :] = kv_ref[c].astype(F32)
        return 0

    lax.fori_loop(0, chunks, place, 0, unroll=4)
    for t in range(chunks * kc // tk):
        kvs_ref[t * tk : (t + 1) * tk, :] = sort_s[t * tk : (t + 1) * tk, :].astype(BF16)
    stage_rows(order_ref, row_refs, q_ref, d_ref, span, hd)

    for half in range(2):

        def score(masked, t, tops):
            keys = pl.ds(pl.multiple_of(t * tk, tk), tk)
            k = kvs_ref[keys, :hd]
            new = []
            for r in parts:
                cols = slice(r * rc, (r + 1) * rc)
                s = lax.dot_general(k, q_ref[half, cols, :], NT, preferred_element_type=F32)
                s = s * factor
                if masked:
                    s = jnp.where(kpos_ref[keys, :] <= qpos_ref[half : half + 1, cols], s, LOW)
                s_s[keys, cols] = s
                new.append(jnp.maximum(tops[r], jnp.max(s.reshape(tk // 8, 8, rc), axis=0)))
            return tuple(new)

        full, count = tiles_ref[2 * half], tiles_ref[2 * half + 1]
        tops = tuple(jnp.full((8, rc), LOW, F32) for _ in parts)
        tops = lax.fori_loop(0, full, functools.partial(score, False), tops)
        tops = lax.fori_loop(full, count, functools.partial(score, True), tops)
        tops = [jnp.max(top, axis=0, keepdims=True) for top in tops]

        def weigh(t, carried):
            keys = pl.ds(pl.multiple_of(t * tk, tk), tk)
            v = kvs_ref[keys, hd:]
            new = []
            for r in parts:
                cols = slice(r * rc, (r + 1) * rc)
                l, ds = carried[r]
                dp = lax.dot_general(v, d_ref[half, cols, :], NT, preferred_element_type=F32)
                p = jnp.exp2(s_s[keys, cols] - tops[r])
                p_s[half, keys, cols] = p.astype(BF16)
                l = l + jnp.sum(p.reshape(tk // 8, 8, rc), axis=0)
                ds = ds + jnp.sum((p * dp).reshape(tk // 8, 8, rc), axis=0)
                new.append((l, ds))
            for copy in tile_copies(pairs, sems, half, t, tk):
                copy.start()
            return tuple(new)

        zero = jnp.zeros((8, rc), F32)
        sums = lax.fori_loop(0, count, weigh, tuple((zero, zero) for _ in parts))
        for r in parts:
            l = jnp.maximum(jnp.sum(sums[r][0], axis=0, keepdims=True), 1e-30)
            ds = jnp.sum(sums[r][1], axis=0, keepdims=True)
            out = columns(half, half_rows, r, rc)
            stat_ref[0:1, out] = tops[r] + jnp.log2(l)
            stat_ref[1:2, out] = ds / l
            stat_ref[2:3, out] = tops[r]
    wait_all(tiles_ref, pairs, sems, tk)


def key_kernel(
    dims, slots_ref, tiles_ref, stat_ref, all_ref, q_ref, d_ref, kvs_ref, probs_ref,
    grads_ref, w_ref, dkv_ref, acc_s, delta_s, p_s, g_s, load_sems, store_sems,
):
    heads, span, hd, chunks, kc, tk, rc = dims
    loads, stores = ((probs_ref, p_s),), ((g_s, grads_ref),)
    start_all(tiles_ref, loads, load_sems, tk)
    scaling = 1.0 / math.sqrt(hd)
    half_rows = heads * span
    parts = range(half_rows // rc)
    acc_s[...] = jnp.zeros_like(acc_s)
    every = [all_ref[h] for h in range(all_ref.shape[0])]
    top = functools.reduce(jnp.maximum, [e[0:1] for e in every])
    weights = [jnp.exp2(e[0:1] - top) for e in every]
    total = functools.reduce(jnp.add, weights)
    weighted = functools.reduce(jnp.add, [w * e[1:2] for w, e in zip(weights, every)])
    w_ref[...] = jnp.exp2(stat_ref[2:3, :] - top - jnp.log2(total))
    delta_s[...] = weighted / total

    for half in range(2):

        def tile(t, _):
            keys = pl.ds(pl.multiple_of(t * tk, tk), tk)
            v = kvs_ref[keys, hd:]
            for copy in tile_copies(loads, load_sems, half, t, tk):
                copy.wait()
            dk = dv = None
            for r in parts:
                cols = slice(r * rc, (r + 1) * rc)
                out = columns(half, half_rows, r, rc)
                q, d = q_ref[half, cols, :], d_ref[half, cols, :]
                p = p_s[half, keys, cols].astype(F32) * w_ref[:, out]
                dp = lax.dot_general(v, d, NT, preferred_element_type=F32)
                g = (p * (dp - delta_s[:, out])).astype(BF16)
                g_s[half, keys, cols] = g
                one = jnp.dot(g, q, preferred_element_type=F32)
                two = jnp.dot(p.astype(BF16), d, preferred_element_type=F32)
                dk, dv = (one, two) if dk is None else (dk + one, dv + two)
            acc_s[keys, :hd] += dk
            acc_s[keys, hd:] += dv
            for copy in tile_copies(stores, store_sems, half, t, tk):
                copy.start()
            return 0

        lax.fori_loop(0, tiles_ref[2 * half + 1], tile, 0)

    def place(c, _):
        start = pl.multiple_of(slots_ref[c] * kc, kc)
        rows = acc_s[pl.ds(start, kc), :]
        dkv_ref[c, :, :hd] = (rows[:, :hd] * scaling).astype(BF16)
        dkv_ref[c, :, hd:] = rows[:, hd:].astype(BF16)
        return 0

    lax.fori_loop(0, chunks, place, 0, unroll=4)
    wait_all(tiles_ref, stores, store_sems, tk)


def row_kernel(dims, tiles_ref, target_ref, w_ref, kvs_ref, probs_ref, grads_ref, *refs):
    heads, span, hd, chunks, kc, tk, rc = dims
    out_refs = refs[:heads]
    o_s, dq_s, kvt_s, flat_s, p_s, g_s, sems = refs[heads:]
    scaling = 1.0 / math.sqrt(hd)
    half_rows = heads * span

    loads = ((probs_ref, p_s), (grads_ref, g_s))
    start_all(tiles_ref, loads, sems, tk)
    for t in range(chunks * kc // tk):
        kvt_s[:, t * tk : (t + 1) * tk] = kvs_ref[t * tk : (t + 1) * tk, :].T
    o_s[...] = jnp.zeros_like(o_s)
    dq_s[...] = jnp.zeros_like(dq_s)
    for half in range(2):

        def tile(t, _):
            keys = pl.ds(pl.multiple_of(t * tk, tk), tk)
            for copy in tile_copies(loads, sems, half, t, tk):
                copy.wait()
            for r in range(half_rows // rc):
                cols = slice(r * rc, (r + 1) * rc)
                out = columns(half, half_rows, r, rc)
                dq_s[:, out] += jnp.dot(
                    kvt_s[:hd, keys], g_s[half, keys, cols], preferred_element_type=F32
                )
                o_s[:, out] += jnp.dot(
                    kvt_s[hd:, keys], p_s[half, keys, cols], preferred_element_type=F32
                )
            return 0

        lax.fori_loop(0, tiles_ref[2 * half + 1], tile, 0)

    blocks = span // kc
    for which, (src, scale) in enumerate(((o_s, w_ref[...]), (dq_s, scaling))):
        flat_s[...] = (src[...] * scale).T
        for number in range(heads):
            target = target_ref[number]
            half, block = target // blocks, target % blocks
            for h in range(heads):
                first = pl.multiple_of(half * half_rows + h * span + block * kc, kc)
                at = which * heads * hd + h * hd
                out_refs[number][:, at : at + hd] = flat_s[pl.ds(first, kc), :].astype(BF16)


def run_stats(dims, slots, tiles, order, kpos, qpos, kv_all, row_parts):
    heads, span, hd, chunks, kc, tk, _ = dims
    half_rows, n_keys = heads * span, chunks * kc
    smem = pl.BlockSpec(memory_space=pltpu.SMEM)
    vmem = pl.BlockSpec(memory_space=pltpu.VMEM)
    hbm = pl.BlockSpec(memory_space=pltpu.HBM)
    return pl.pallas_call(
        functools.partial(stats_kernel, dims),
        out_shape=(
            jax.ShapeDtypeStruct((3, 2 * half_rows), F32),
            jax.ShapeDtypeStruct((n_keys, 2 * hd), BF16),
            jax.ShapeDtypeStruct((2, half_rows, hd), BF16),
            jax.ShapeDtypeStruct((2, half_rows, hd), BF16),
            jax.ShapeDtypeStruct((2, n_keys, half_rows), BF16),
        ),
        in_specs=[smem] * 3 + [vmem] * (3 + heads),
        out_specs=(vmem,) * 4 + (hbm,),
        scratch_shapes=[
            pltpu.VMEM((n_keys, half_rows), F32),
            pltpu.VMEM((n_keys, 2 * hd), F32),
            pltpu.VMEM((2, n_keys, half_rows), BF16),
            pltpu.SemaphoreType.DMA((1, 2, n_keys // tk)),
        ],
        compiler_params=pltpu.CompilerParams(vmem_limit_bytes=48 * 1024 * 1024),
        name="attention_stats",
    )(slots, tiles, order, kpos, qpos, kv_all, *row_parts)


def run_keys(dims, slots, tiles, stat, stat_all, q, d, kvs, probs):
    heads, span, hd, chunks, kc, tk, _ = dims
    rows, n_keys = 2 * heads * span, chunks * kc
    smem = pl.BlockSpec(memory_space=pltpu.SMEM)
    vmem = pl.BlockSpec(memory_space=pltpu.VMEM)
    hbm = pl.BlockSpec(memory_space=pltpu.HBM)
    return pl.pallas_call(
        functools.partial(key_kernel, dims),
        out_shape=(
            jax.ShapeDtypeStruct((2, n_keys, rows // 2), BF16),
            jax.ShapeDtypeStruct((1, rows), F32),
            jax.ShapeDtypeStruct((chunks, kc, 2 * hd), BF16),
        ),
        in_specs=[smem] * 2 + [vmem] * 5 + [hbm],
        out_specs=(hbm, vmem, vmem),
        scratch_shapes=[
            pltpu.VMEM((n_keys, 2 * hd), F32),
            pltpu.VMEM((1, rows), F32),
            pltpu.VMEM((2, n_keys, rows // 2), BF16),
            pltpu.VMEM((2, n_keys, rows // 2), BF16),
            pltpu.SemaphoreType.DMA((1, 2, n_keys // tk)),
            pltpu.SemaphoreType.DMA((1, 2, n_keys // tk)),
        ],
        compiler_params=pltpu.CompilerParams(vmem_limit_bytes=48 * 1024 * 1024),
        cost_estimate=pl.CostEstimate(
            flops=3 * n_keys * rows * hd, bytes_accessed=8 * n_keys * rows, transcendentals=0
        ),
        name="attention_keys",
    )(slots, tiles, stat, stat_all, q, d, kvs, probs)


def run_rows(dims, tiles, targets, weights, kvs, probs, grads):
    heads, span, hd, chunks, kc, tk, _ = dims
    rows, n_keys = 2 * heads * span, chunks * kc
    smem = pl.BlockSpec(memory_space=pltpu.SMEM)
    vmem = pl.BlockSpec(memory_space=pltpu.VMEM)
    hbm = pl.BlockSpec(memory_space=pltpu.HBM)
    return pl.pallas_call(
        functools.partial(row_kernel, dims),
        out_shape=(jax.ShapeDtypeStruct((kc, 2 * heads * hd), BF16),) * heads,
        in_specs=[smem] * 2 + [vmem] * 2 + [hbm] * 2,
        out_specs=(vmem,) * heads,
        scratch_shapes=[
            pltpu.VMEM((hd, rows), F32),
            pltpu.VMEM((hd, rows), F32),
            pltpu.VMEM((2 * hd, n_keys), BF16),
            pltpu.VMEM((rows, hd), F32),
            pltpu.VMEM((2, n_keys, rows // 2), BF16),
            pltpu.VMEM((2, n_keys, rows // 2), BF16),
            pltpu.SemaphoreType.DMA((2, 2, n_keys // tk)),
        ],
        compiler_params=pltpu.CompilerParams(vmem_limit_bytes=48 * 1024 * 1024),
        cost_estimate=pl.CostEstimate(
            flops=n_keys * rows * hd, bytes_accessed=2 * n_keys * rows, transcendentals=0
        ),
        name="attention_rows",
    )(tiles, targets, weights, kvs, probs, grads)


def exchange(x, axis):
    return lax.all_to_all(x, axis, split_axis=0, concat_axis=0, tiled=True)


def send(x, mesh_x, step, cross):
    pairs = [
        (2 * a + c, 2 * ((a + step) % mesh_x) + (c ^ cross))
        for a in range(mesh_x)
        for c in range(2)
    ]
    return lax.ppermute(x, "head", pairs)


def local(query_in, key_in, value_in, grad_out, span_of):
    hd = key_in.shape[1]
    kc = key_in.shape[0]
    heads = lax.axis_size("head")
    shards = lax.axis_size("ctx")
    local_rows = query_in.shape[0]
    span = local_rows // 2
    n_keys = shards * kc
    tk = math.gcd(n_keys, 256)
    rc = heads * span
    dims = (heads, span, hd, shards, kc, tk, rc)
    blocks = span // kc
    ctx = lax.axis_index("ctx")
    head = lax.axis_index("head")

    mesh_x = heads // 2
    at_x, core = head // 2, head % 2
    moves = [(step, cross) for step in range(mesh_x) for cross in range(2)]
    order = jnp.stack(
        [lax.rem(at_x - step + mesh_x, mesh_x) * 2 + (core ^ cross) for step, cross in moves]
    )
    targets = jnp.stack(
        [lax.rem(at_x + step, mesh_x) * 2 + (core ^ cross) for step, cross in moves]
    )

    spans = span_of.reshape(shards, 2)
    key_span = lax.dynamic_index_in_dim(spans, head // blocks, 1, keepdims=False)
    own = lax.dynamic_index_in_dim(spans, ctx, 0, keepdims=False)
    rank = jnp.sum((key_span[None, :] < key_span[:, None]).astype(jnp.int32), axis=1)
    place = jnp.arange(shards, dtype=jnp.int32)
    ordered = jnp.sum(jnp.where(rank[None, :] == place[:, None], key_span[None, :], 0), axis=1)
    kpos = (
        ordered[:, None] * span
        + (head % blocks) * kc
        + jnp.arange(kc, dtype=jnp.int32)[None, :]
    ).reshape(n_keys, 1)
    qpos = own[:, None] * span + jnp.tile(jnp.arange(span, dtype=jnp.int32), heads)[None, :]
    before = jnp.sum((key_span[None, :] < own[:, None]).astype(jnp.int32), axis=1) * kc
    seen = jnp.sum((key_span[None, :] <= own[:, None]).astype(jnp.int32), axis=1) * kc
    tiles = jnp.stack([before // tk, (seen + tk - 1) // tk], axis=1).reshape(4)

    kv = jnp.concatenate([key_in, value_in], axis=1)
    qd = jnp.concatenate([query_in, grad_out], axis=1)
    kv_all = exchange(jnp.broadcast_to(kv[None], (shards, kc, 2 * hd)), "ctx")
    row_parts = [qd] + [send(qd, mesh_x, step, cross) for step, cross in moves[1:]]

    stat, kvs, q, d, probs = run_stats(dims, rank, tiles, order, kpos, qpos, kv_all, row_parts)
    rows = 2 * heads * span
    stat_all = exchange(jnp.broadcast_to(stat[None, :2], (heads, 2, rows)), "head")
    grads, weights, key_parts = run_keys(dims, rank, tiles, stat, stat_all, q, d, kvs, probs)
    key_parts = exchange(key_parts, "ctx")
    row_parts = run_rows(dims, tiles, targets, weights, kvs, probs, grads)
    row_sum = row_parts[0].astype(F32)
    for (step, cross), part in zip(moves[1:], row_parts[1:]):
        row_sum = row_sum + send(part, mesh_x, step, cross).astype(F32)
    row_sum = row_sum.astype(BF16)
    key_sum = jnp.sum(key_parts.astype(F32), axis=0).astype(BF16)
    width = heads * hd
    return (row_sum[:, :width], row_sum[:, width:], key_sum[:, :hd], key_sum[:, hd:])


def solution(mesh):
    return jax.shard_map(
        local,
        mesh=mesh,
        in_specs=(
            P("ctx", "head"),
            P(("ctx", "head"), None),
            P(("ctx", "head"), None),
            P("ctx", "head"),
            P(),
        ),
        out_specs=(P(("ctx", "head"), None),) * 4,
        check_vma=False,
    )
```

```python
import functools
import math

import jax
import jax.numpy as jnp
from jax import lax
from jax.experimental import pallas as pl
from jax.experimental.pallas import tpu as pltpu
from jax.sharding import PartitionSpec as P

F32 = jnp.float32
BF16 = jnp.bfloat16
LOG2E = 1.4426950408889634
LOW = -1e30
NT = (((1,), (1,)), ((), ()))


def stage_rows(order_ref, sources, q_ref, d_ref, span, hd):
    number = 0
    for src_ref in sources:
        for piece in range(src_ref.shape[0]):
            at = pl.ds(pl.multiple_of(order_ref[number] * span, span), span)
            for half in range(2):
                rows = src_ref[piece, half * span : (half + 1) * span, :]
                q_ref[half, at, :] = rows[:, :hd]
                d_ref[half, at, :] = rows[:, hd:]
            number += 1


def columns(half, half_rows, r, rc):
    first = half * half_rows + r * rc
    return slice(first, first + rc)


def stats_kernel(
    dims, slots_ref, tiles_ref, order_ref, kpos_ref, qpos_ref, near_ref, far_ref, kv_ref,
    stat_ref, kvs_ref, q_ref, d_ref, p_ref, s_s, sort_s,
):
    heads, span, hd, chunks, kc, tk, rc = dims
    factor = LOG2E / math.sqrt(hd)
    half_rows = heads * span
    parts = range(half_rows // rc)

    def place(c, _):
        start = pl.multiple_of(slots_ref[c] * kc, kc)
        sort_s[pl.ds(start, kc), :] = kv_ref[c].astype(F32)
        return 0

    lax.fori_loop(0, chunks, place, 0, unroll=4)
    for t in range(chunks * kc // tk):
        kvs_ref[t * tk : (t + 1) * tk, :] = sort_s[t * tk : (t + 1) * tk, :].astype(BF16)
    stage_rows(order_ref, (near_ref, far_ref), q_ref, d_ref, span, hd)

    for half in range(2):

        def score(masked, t, tops):
            keys = pl.ds(pl.multiple_of(t * tk, tk), tk)
            k = kvs_ref[keys, :hd]
            new = []
            for r in parts:
                cols = slice(r * rc, (r + 1) * rc)
                s = lax.dot_general(k, q_ref[half, cols, :], NT, preferred_element_type=F32)
                s = s * factor
                if masked:
                    s = jnp.where(kpos_ref[keys, :] <= qpos_ref[half : half + 1, cols], s, LOW)
                s_s[keys, cols] = s
                new.append(jnp.maximum(tops[r], jnp.max(s.reshape(tk // 8, 8, rc), axis=0)))
            return tuple(new)

        full, count = tiles_ref[2 * half], tiles_ref[2 * half + 1]
        tops = tuple(jnp.full((8, rc), LOW, F32) for _ in parts)
        tops = lax.fori_loop(0, full, functools.partial(score, False), tops)
        tops = lax.fori_loop(full, count, functools.partial(score, True), tops)
        tops = [jnp.max(top, axis=0, keepdims=True) for top in tops]

        def weigh(t, carried):
            keys = pl.ds(pl.multiple_of(t * tk, tk), tk)
            v = kvs_ref[keys, hd:]
            new = []
            for r in parts:
                cols = slice(r * rc, (r + 1) * rc)
                l, ds = carried[r]
                dp = lax.dot_general(v, d_ref[half, cols, :], NT, preferred_element_type=F32)
                p = jnp.exp2(s_s[keys, cols] - tops[r])
                p_ref[keys, columns(half, half_rows, r, rc)] = p.astype(BF16)
                l = l + jnp.sum(p.reshape(tk // 8, 8, rc), axis=0)
                ds = ds + jnp.sum((p * dp).reshape(tk // 8, 8, rc), axis=0)
                new.append((l, ds))
            return tuple(new)

        zero = jnp.zeros((8, rc), F32)
        sums = lax.fori_loop(0, count, weigh, tuple((zero, zero) for _ in parts))
        for r in parts:
            l = jnp.maximum(jnp.sum(sums[r][0], axis=0, keepdims=True), 1e-30)
            ds = jnp.sum(sums[r][1], axis=0, keepdims=True)
            out = columns(half, half_rows, r, rc)
            stat_ref[0:1, out] = tops[r] + jnp.log2(l)
            stat_ref[1:2, out] = ds / l
            stat_ref[2:3, out] = tops[r]


def grad_kernel(
    dims, slots_ref, tiles_ref, order_ref, stat_ref, all_ref, q_ref, d_ref, kvs_ref, p_ref,
    keep_ref, send_ref, dkv_ref, acc_s, o_s, dq_s, kvt_s, w_s, delta_s, flat_s,
):
    heads, span, hd, chunks, kc, tk, rc = dims
    scaling = 1.0 / math.sqrt(hd)
    half_rows = heads * span
    parts = range(half_rows // rc)
    for t in range(chunks * kc // tk):
        kvt_s[:, t * tk : (t + 1) * tk] = kvs_ref[t * tk : (t + 1) * tk, :].T
    acc_s[...] = jnp.zeros_like(acc_s)
    o_s[...] = jnp.zeros_like(o_s)
    dq_s[...] = jnp.zeros_like(dq_s)
    every = [all_ref[h] for h in range(all_ref.shape[0])]
    top = functools.reduce(jnp.maximum, [e[0:1] for e in every])
    weights = [jnp.exp2(e[0:1] - top) for e in every]
    total = functools.reduce(jnp.add, weights)
    weighted = functools.reduce(jnp.add, [w * e[1:2] for w, e in zip(weights, every)])
    w_s[...] = jnp.exp2(stat_ref[2:3, :] - top - jnp.log2(total))
    delta_s[...] = weighted / total
    for half in range(2):

        def tile(t, _):
            keys = pl.ds(pl.multiple_of(t * tk, tk), tk)
            v = kvs_ref[keys, hd:]
            dk = dv = None
            for r in parts:
                cols = slice(r * rc, (r + 1) * rc)
                out = columns(half, half_rows, r, rc)
                q, d = q_ref[half, cols, :], d_ref[half, cols, :]
                p = p_ref[keys, out].astype(F32) * w_s[:, out]
                dp = lax.dot_general(v, d, NT, preferred_element_type=F32)
                pb = p.astype(BF16)
                g = (p * (dp - delta_s[:, out])).astype(BF16)
                one = jnp.dot(g, q, preferred_element_type=F32)
                two = jnp.dot(pb, d, preferred_element_type=F32)
                dk, dv = (one, two) if dk is None else (dk + one, dv + two)
                dq_s[:, out] += jnp.dot(kvt_s[:hd, keys], g, preferred_element_type=F32)
                o_s[:, out] += jnp.dot(kvt_s[hd:, keys], pb, preferred_element_type=F32)
            acc_s[keys, :hd] += dk
            acc_s[keys, hd:] += dv
            return 0

        lax.fori_loop(0, tiles_ref[2 * half + 1], tile, 0)

    def place(c, _):
        start = pl.multiple_of(slots_ref[c] * kc, kc)
        rows = acc_s[pl.ds(start, kc), :]
        dkv_ref[c, :, :hd] = (rows[:, :hd] * scaling).astype(BF16)
        dkv_ref[c, :, hd:] = rows[:, hd:].astype(BF16)
        return 0

    lax.fori_loop(0, chunks, place, 0, unroll=4)
    blocks = span // kc
    per_core = heads // 2
    for which, (src, scale) in enumerate(((o_s, 1.0), (dq_s, scaling))):
        flat_s[...] = (src[...] * scale).T
        for number in range(heads):
            target = order_ref[number]
            half, block = target // blocks, target % blocks
            out_ref = keep_ref if number < per_core else send_ref
            for h in range(heads):
                first = pl.multiple_of(half * half_rows + h * span + block * kc, kc)
                at = which * heads * hd + h * hd
                out_ref[number % per_core, :, at : at + hd] = flat_s[
                    pl.ds(first, kc), :
                ].astype(BF16)


def pack_kernel(hd, q_ref, d_ref, k_ref, v_ref, qd_ref, kv_ref, sems):
    pairs = ((q_ref, qd_ref.at[0, :, :hd]), (d_ref, qd_ref.at[0, :, hd:]))
    copies = [pltpu.make_async_copy(a, b, sems.at[n]) for n, (a, b) in enumerate(pairs)]
    for copy in copies:
        copy.start()
    shape = kv_ref.shape[:2] + (hd,)
    kv_ref[:, :, :hd] = jnp.broadcast_to(k_ref[...][None], shape)
    kv_ref[:, :, hd:] = jnp.broadcast_to(v_ref[...][None], shape)
    for copy in copies:
        copy.wait()


def run_pack(shards, query, dout, key, value):
    (rows, hd), kc = query.shape, key.shape[0]
    return pl.pallas_call(
        functools.partial(pack_kernel, hd),
        out_shape=(
            jax.ShapeDtypeStruct((1, rows, 2 * hd), BF16),
            jax.ShapeDtypeStruct((shards, kc, 2 * hd), BF16),
        ),
        in_specs=[pl.BlockSpec(memory_space=pltpu.HBM)] * 2
        + [pl.BlockSpec(memory_space=pltpu.VMEM)] * 2,
        scratch_shapes=[pltpu.SemaphoreType.DMA((2,))],
        compiler_params=pltpu.CompilerParams(vmem_limit_bytes=63 * 1024 * 1024),
        name="attention_pack",
    )(query, dout, key, value)


def run_stats(dims, slots, tiles, order, kpos, qpos, near, far, kv_all):
    heads, span, hd, chunks, kc, _, _ = dims
    half_rows, n_keys = heads * span, chunks * kc
    smem = pl.BlockSpec(memory_space=pltpu.SMEM)
    vmem = pl.BlockSpec(memory_space=pltpu.VMEM)
    return pl.pallas_call(
        functools.partial(stats_kernel, dims),
        out_shape=(
            jax.ShapeDtypeStruct((3, 2 * half_rows), F32),
            jax.ShapeDtypeStruct((n_keys, 2 * hd), BF16),
            jax.ShapeDtypeStruct((2, half_rows, hd), BF16),
            jax.ShapeDtypeStruct((2, half_rows, hd), BF16),
            jax.ShapeDtypeStruct((n_keys, 2 * half_rows), BF16),
        ),
        in_specs=[smem] * 3 + [vmem] * 5,
        out_specs=(vmem,) * 5,
        scratch_shapes=[
            pltpu.VMEM((n_keys, half_rows), F32),
            pltpu.VMEM((n_keys, 2 * hd), F32),
        ],
        compiler_params=pltpu.CompilerParams(vmem_limit_bytes=32 * 1024 * 1024),
        name="attention_stats",
    )(slots, tiles, order, kpos, qpos, near, far, kv_all)


def run_grads(dims, slots, tiles, order, stat, stat_all, q, d, kvs, probs):
    heads, span, hd, chunks, kc, _, _ = dims
    rows, n_keys = 2 * heads * span, chunks * kc
    smem = pl.BlockSpec(memory_space=pltpu.SMEM)
    vmem = pl.BlockSpec(memory_space=pltpu.VMEM)
    return pl.pallas_call(
        functools.partial(grad_kernel, dims),
        out_shape=(
            jax.ShapeDtypeStruct((heads // 2, kc, 2 * heads * hd), BF16),
            jax.ShapeDtypeStruct((heads // 2, kc, 2 * heads * hd), BF16),
            jax.ShapeDtypeStruct((chunks, kc, 2 * hd), BF16),
        ),
        in_specs=[smem] * 3 + [vmem] * 6,
        out_specs=(vmem,) * 3,
        scratch_shapes=[
            pltpu.VMEM((n_keys, 2 * hd), F32),
            pltpu.VMEM((hd, rows), F32),
            pltpu.VMEM((hd, rows), F32),
            pltpu.VMEM((2 * hd, n_keys), BF16),
            pltpu.VMEM((1, rows), F32),
            pltpu.VMEM((1, rows), F32),
            pltpu.VMEM((rows, hd), F32),
        ],
        compiler_params=pltpu.CompilerParams(vmem_limit_bytes=32 * 1024 * 1024),
        name="attention_grads",
    )(slots, tiles, order, stat, stat_all, q, d, kvs, probs)


def exchange(x, axis):
    return lax.all_to_all(x, axis, split_axis=0, concat_axis=0, tiled=True)


def flip_x(x, mesh_x, mask):
    pairs = [(2 * a + c, 2 * (a ^ mask) + c) for a in range(mesh_x) for c in range(2)]
    return lax.ppermute(x, "head", pairs)


def swap_cores(x, mesh_x):
    pairs = [(2 * a + c, 2 * a + 1 - c) for a in range(mesh_x) for c in range(2)]
    return lax.ppermute(x, "head", pairs)


def local(query_in, key_in, value_in, grad_out, span_of):
    hd = key_in.shape[1]
    kc = key_in.shape[0]
    heads = lax.axis_size("head")
    shards = lax.axis_size("ctx")
    local_rows = query_in.shape[0]
    span = local_rows // 2
    n_keys = shards * kc
    tk = math.gcd(n_keys, 256)
    rc = heads * span
    dims = (heads, span, hd, shards, kc, tk, rc)
    blocks = span // kc
    ctx = lax.axis_index("ctx")
    head = lax.axis_index("head")

    mesh_x = heads // 2
    at_x, core = head // 2, head % 2
    masks = [2 ** (bit + 1) - 1 for bit in range(mesh_x.bit_length() - 1)]
    offsets = [0]
    for mask in masks:
        offsets = offsets + [mask ^ offset for offset in offsets]
    origin = jnp.bitwise_xor(at_x, jnp.array(offsets, jnp.int32)) * 2
    order = jnp.concatenate([origin + core, origin + 1 - core]).astype(jnp.int32)

    spans = span_of.reshape(shards, 2)
    key_span = lax.dynamic_index_in_dim(spans, head // blocks, 1, keepdims=False)
    own = lax.dynamic_index_in_dim(spans, ctx, 0, keepdims=False)
    rank = jnp.sum((key_span[None, :] < key_span[:, None]).astype(jnp.int32), axis=1)
    place = jnp.arange(shards, dtype=jnp.int32)
    ordered = jnp.sum(jnp.where(rank[None, :] == place[:, None], key_span[None, :], 0), axis=1)
    kpos = (
        ordered[:, None] * span
        + (head % blocks) * kc
        + jnp.arange(kc, dtype=jnp.int32)[None, :]
    ).reshape(n_keys, 1)
    qpos = own[:, None] * span + jnp.tile(jnp.arange(span, dtype=jnp.int32), heads)[None, :]
    before = jnp.sum((key_span[None, :] < own[:, None]).astype(jnp.int32), axis=1) * kc
    seen = jnp.sum((key_span[None, :] <= own[:, None]).astype(jnp.int32), axis=1) * kc
    tiles = jnp.stack([before // tk, (seen + tk - 1) // tk], axis=1).reshape(4)

    near, kv_all = run_pack(shards, query_in, grad_out, key_in, value_in)
    kv_all = exchange(kv_all, "ctx")
    for mask in masks:
        near = jnp.concatenate([near, flip_x(near, mesh_x, mask)])
    far = swap_cores(near, mesh_x)

    stat, kvs, q, d, probs = run_stats(dims, rank, tiles, order, kpos, qpos, near, far, kv_all)
    rows = 2 * heads * span
    stat_all = exchange(jnp.broadcast_to(stat[None, :2], (heads, 2, rows)), "head")
    keep, send, key_parts = run_grads(
        dims, rank, tiles, order, stat, stat_all, q, d, kvs, probs
    )
    key_parts = exchange(key_parts, "ctx")

    row_sum = keep.astype(F32) + swap_cores(send, mesh_x).astype(F32)
    for mask in reversed(masks):
        half = row_sum.shape[0] // 2
        moved = flip_x(row_sum[half:].astype(BF16), mesh_x, mask)
        row_sum = row_sum[:half] + moved.astype(F32)
    row_sum = row_sum[0].astype(BF16)
    key_sum = jnp.sum(key_parts.astype(F32), axis=0).astype(BF16)
    width = heads * hd
    return (row_sum[:, :width], row_sum[:, width:], key_sum[:, :hd], key_sum[:, hd:])


def solution(mesh):
    return jax.shard_map(
        local,
        mesh=mesh,
        in_specs=(
            P("ctx", "head"),
            P(("ctx", "head"), None),
            P(("ctx", "head"), None),
            P("ctx", "head"),
            P(),
        ),
        out_specs=(P(("ctx", "head"), None),) * 4,
        check_vma=False,
    )
```

```python
import functools
import math

import jax
import jax.numpy as jnp
from jax import lax
from jax.experimental import pallas as pl
from jax.experimental.pallas import tpu as pltpu
from jax.sharding import PartitionSpec as P

F32 = jnp.float32
BF16 = jnp.bfloat16
LOG2E = 1.4426950408889634
LOW = -1e30
NT = (((1,), (1,)), ((), ()))


def flips(mesh_x):
    masks = [2 ** (bit + 1) - 1 for bit in range(mesh_x.bit_length() - 1)]
    offsets = [0]
    for mask in masks:
        offsets = offsets + [mask ^ offset for offset in offsets]
    return masks, offsets


def partner(number, heads):
    mesh_x = heads // 2
    head = lax.axis_index("head")
    _, offsets = flips(mesh_x)
    change = 2 * offsets[number % mesh_x] + number // mesh_x
    return jnp.bitwise_xor(head, jnp.int32(change))


def stage_rows(sources, q_ref, d_ref, heads, span, hd):
    number = 0
    for src_ref in sources:
        for piece in range(src_ref.shape[0]):
            at = pl.ds(pl.multiple_of(partner(number, heads) * span, span), span)
            for half in range(2):
                rows = src_ref[piece, half * span : (half + 1) * span, :]
                q_ref[half, at, :] = rows[:, :hd]
                d_ref[half, at, :] = rows[:, hd:]
            number += 1


def columns(half, half_rows, r, rc):
    first = half * half_rows + r * rc
    return slice(first, first + rc)


def stats_kernel(
    dims, slots_ref, full_ref, count_ref, kpos_ref, qpos_ref, near_ref, far_ref, kv_ref,
    stat_ref, kvs_ref, q_ref, d_ref, p_ref, s_s, sort_s,
):
    heads, span, hd, chunks, kc, tk, rc = dims
    factor = LOG2E / math.sqrt(hd)
    half_rows = heads * span
    parts = range(half_rows // rc)

    part = lax.axis_index("head") // (span // kc)

    def place(c, _):
        start = pl.multiple_of(slots_ref[2 * c + part] * kc, kc)
        sort_s[pl.ds(start, kc), :] = kv_ref[c].astype(F32)
        return 0

    lax.fori_loop(0, chunks, place, 0, unroll=4)
    for t in range(chunks * kc // tk):
        kvs_ref[t * tk : (t + 1) * tk, :] = sort_s[t * tk : (t + 1) * tk, :].astype(BF16)
    stage_rows((near_ref, far_ref), q_ref, d_ref, heads, span, hd)

    for half in range(2):

        def score(masked, t, tops):
            keys = pl.ds(pl.multiple_of(t * tk, tk), tk)
            k = kvs_ref[keys, :hd]
            new = []
            for r in parts:
                cols = slice(r * rc, (r + 1) * rc)
                s = lax.dot_general(k, q_ref[half, cols, :], NT, preferred_element_type=F32)
                s = s * factor
                if masked:
                    s = jnp.where(kpos_ref[keys, :] <= qpos_ref[half : half + 1, cols], s, LOW)
                s_s[keys, cols] = s
                new.append(jnp.maximum(tops[r], jnp.max(s.reshape(tk // 8, 8, rc), axis=0)))
            return tuple(new)

        full, count = full_ref[half], count_ref[half]
        tops = tuple(jnp.full((8, rc), LOW, F32) for _ in parts)
        tops = lax.fori_loop(0, full, functools.partial(score, False), tops)
        tops = lax.fori_loop(full, count, functools.partial(score, True), tops)
        tops = [jnp.max(top, axis=0, keepdims=True) for top in tops]

        def weigh(t, carried):
            keys = pl.ds(pl.multiple_of(t * tk, tk), tk)
            v = kvs_ref[keys, hd:]
            new = []
            for r in parts:
                cols = slice(r * rc, (r + 1) * rc)
                l, ds = carried[r]
                dp = lax.dot_general(v, d_ref[half, cols, :], NT, preferred_element_type=F32)
                p = jnp.exp2(s_s[keys, cols] - tops[r])
                p_ref[keys, columns(half, half_rows, r, rc)] = p.astype(BF16)
                l = l + jnp.sum(p.reshape(tk // 8, 8, rc), axis=0)
                ds = ds + jnp.sum((p * dp).reshape(tk // 8, 8, rc), axis=0)
                new.append((l, ds))
            return tuple(new)

        zero = jnp.zeros((8, rc), F32)
        sums = lax.fori_loop(0, count, weigh, tuple((zero, zero) for _ in parts))
        for r in parts:
            l = jnp.maximum(jnp.sum(sums[r][0], axis=0, keepdims=True), 1e-30)
            ds = jnp.sum(sums[r][1], axis=0, keepdims=True)
            out = columns(half, half_rows, r, rc)
            stat_ref[0:1, out] = tops[r] + jnp.log2(l)
            stat_ref[1:2, out] = ds / l
            stat_ref[2:3, out] = tops[r]


def grad_kernel(
    dims, slots_ref, full_ref, count_ref, stat_ref, all_ref, q_ref, d_ref, kvs_ref, p_ref,
    keep_ref, send_ref, dkv_ref, acc_s, o_s, dq_s, kvt_s, w_s, delta_s, flat_s,
):
    heads, span, hd, chunks, kc, tk, rc = dims
    scaling = 1.0 / math.sqrt(hd)
    half_rows = heads * span
    parts = range(half_rows // rc)
    for t in range(chunks * kc // tk):
        kvt_s[:, t * tk : (t + 1) * tk] = kvs_ref[t * tk : (t + 1) * tk, :].T
    acc_s[...] = jnp.zeros_like(acc_s)
    o_s[...] = jnp.zeros_like(o_s)
    dq_s[...] = jnp.zeros_like(dq_s)
    every = [all_ref[h] for h in range(all_ref.shape[0])]
    top = functools.reduce(jnp.maximum, [e[0:1] for e in every])
    weights = [jnp.exp2(e[0:1] - top) for e in every]
    total = functools.reduce(jnp.add, weights)
    weighted = functools.reduce(jnp.add, [w * e[1:2] for w, e in zip(weights, every)])
    w_s[...] = jnp.exp2(stat_ref[2:3, :] - top - jnp.log2(total))
    delta_s[...] = weighted / total
    for half in range(2):

        def tile(t, _):
            keys = pl.ds(pl.multiple_of(t * tk, tk), tk)
            v = kvs_ref[keys, hd:]
            dk = dv = None
            for r in parts:
                cols = slice(r * rc, (r + 1) * rc)
                out = columns(half, half_rows, r, rc)
                q, d = q_ref[half, cols, :], d_ref[half, cols, :]
                p = p_ref[keys, out].astype(F32) * w_s[:, out]
                dp = lax.dot_general(v, d, NT, preferred_element_type=F32)
                pb = p.astype(BF16)
                g = (p * (dp - delta_s[:, out])).astype(BF16)
                one = jnp.dot(g, q, preferred_element_type=F32)
                two = jnp.dot(pb, d, preferred_element_type=F32)
                dk, dv = (one, two) if dk is None else (dk + one, dv + two)
                dq_s[:, out] += jnp.dot(kvt_s[:hd, keys], g, preferred_element_type=F32)
                o_s[:, out] += jnp.dot(kvt_s[hd:, keys], pb, preferred_element_type=F32)
            acc_s[keys, :hd] += dk
            acc_s[keys, hd:] += dv
            return 0

        lax.fori_loop(0, count_ref[half], tile, 0)

    part = lax.axis_index("head") // (span // kc)

    def place(c, _):
        start = pl.multiple_of(slots_ref[2 * c + part] * kc, kc)
        rows = acc_s[pl.ds(start, kc), :]
        dkv_ref[c, :, :hd] = (rows[:, :hd] * scaling).astype(BF16)
        dkv_ref[c, :, hd:] = rows[:, hd:].astype(BF16)
        return 0

    lax.fori_loop(0, chunks, place, 0, unroll=4)
    blocks = span // kc
    per_core = heads // 2
    for which, (src, scale) in enumerate(((o_s, 1.0), (dq_s, scaling))):
        flat_s[...] = (src[...] * scale).T
        for number in range(heads):
            target = partner(number, heads)
            half, block = target // blocks, target % blocks
            out_ref = keep_ref if number < per_core else send_ref
            for h in range(heads):
                first = pl.multiple_of(half * half_rows + h * span + block * kc, kc)
                at = which * heads * hd + h * hd
                out_ref[number % per_core, :, at : at + hd] = flat_s[
                    pl.ds(first, kc), :
                ].astype(BF16)


def pack_kernel(hd, q_ref, d_ref, k_ref, v_ref, qd_ref, kv_ref, sems):
    pairs = ((q_ref, qd_ref.at[0, :, :hd]), (d_ref, qd_ref.at[0, :, hd:]))
    copies = [pltpu.make_async_copy(a, b, sems.at[n]) for n, (a, b) in enumerate(pairs)]
    for copy in copies:
        copy.start()
    shape = kv_ref.shape[:2] + (hd,)
    kv_ref[:, :, :hd] = jnp.broadcast_to(k_ref[...][None], shape)
    kv_ref[:, :, hd:] = jnp.broadcast_to(v_ref[...][None], shape)
    for copy in copies:
        copy.wait()


def run_pack(shards, query, dout, key, value):
    (rows, hd), kc = query.shape, key.shape[0]
    return pl.pallas_call(
        functools.partial(pack_kernel, hd),
        out_shape=(
            jax.ShapeDtypeStruct((1, rows, 2 * hd), BF16),
            jax.ShapeDtypeStruct((shards, kc, 2 * hd), BF16),
        ),
        in_specs=[pl.BlockSpec(memory_space=pltpu.HBM)] * 2
        + [pl.BlockSpec(memory_space=pltpu.VMEM)] * 2,
        scratch_shapes=[pltpu.SemaphoreType.DMA((2,))],
        compiler_params=pltpu.CompilerParams(vmem_limit_bytes=63 * 1024 * 1024),
        name="attention_pack",
    )(query, dout, key, value)


def run_stats(dims, slots, full, count, kpos, qpos, near, far, kv_all):
    heads, span, hd, chunks, kc, _, _ = dims
    half_rows, n_keys = heads * span, chunks * kc
    smem = pl.BlockSpec(memory_space=pltpu.SMEM)
    vmem = pl.BlockSpec(memory_space=pltpu.VMEM)
    return pl.pallas_call(
        functools.partial(stats_kernel, dims),
        out_shape=(
            jax.ShapeDtypeStruct((3, 2 * half_rows), F32),
            jax.ShapeDtypeStruct((n_keys, 2 * hd), BF16),
            jax.ShapeDtypeStruct((2, half_rows, hd), BF16),
            jax.ShapeDtypeStruct((2, half_rows, hd), BF16),
            jax.ShapeDtypeStruct((n_keys, 2 * half_rows), BF16),
        ),
        in_specs=[smem] * 3 + [vmem] * 5,
        out_specs=(vmem,) * 5,
        scratch_shapes=[
            pltpu.VMEM((n_keys, half_rows), F32),
            pltpu.VMEM((n_keys, 2 * hd), F32),
        ],
        compiler_params=pltpu.CompilerParams(vmem_limit_bytes=32 * 1024 * 1024),
        name="attention_stats",
    )(slots, full, count, kpos, qpos, near, far, kv_all)


def run_grads(dims, slots, full, count, stat, stat_all, q, d, kvs, probs):
    heads, span, hd, chunks, kc, _, _ = dims
    rows, n_keys = 2 * heads * span, chunks * kc
    smem = pl.BlockSpec(memory_space=pltpu.SMEM)
    vmem = pl.BlockSpec(memory_space=pltpu.VMEM)
    return pl.pallas_call(
        functools.partial(grad_kernel, dims),
        out_shape=(
            jax.ShapeDtypeStruct((heads // 2, kc, 2 * heads * hd), BF16),
            jax.ShapeDtypeStruct((heads // 2, kc, 2 * heads * hd), BF16),
            jax.ShapeDtypeStruct((chunks, kc, 2 * hd), BF16),
        ),
        in_specs=[smem] * 3 + [vmem] * 6,
        out_specs=(vmem,) * 3,
        scratch_shapes=[
            pltpu.VMEM((n_keys, 2 * hd), F32),
            pltpu.VMEM((hd, rows), F32),
            pltpu.VMEM((hd, rows), F32),
            pltpu.VMEM((2 * hd, n_keys), BF16),
            pltpu.VMEM((1, rows), F32),
            pltpu.VMEM((1, rows), F32),
            pltpu.VMEM((rows, hd), F32),
        ],
        compiler_params=pltpu.CompilerParams(vmem_limit_bytes=32 * 1024 * 1024),
        name="attention_grads",
    )(slots, full, count, stat, stat_all, q, d, kvs, probs)


def exchange(x, axis):
    return lax.all_to_all(x, axis, split_axis=0, concat_axis=0, tiled=True)


def flip_x(x, mesh_x, mask):
    pairs = [(2 * a + c, 2 * (a ^ mask) + c) for a in range(mesh_x) for c in range(2)]
    return lax.ppermute(x, "head", pairs)


def swap_cores(x, mesh_x):
    pairs = [(2 * a + c, 2 * a + 1 - c) for a in range(mesh_x) for c in range(2)]
    return lax.ppermute(x, "head", pairs)


def local(query_in, key_in, value_in, grad_out, span_of):
    hd = key_in.shape[1]
    kc = key_in.shape[0]
    heads = lax.axis_size("head")
    shards = lax.axis_size("ctx")
    local_rows = query_in.shape[0]
    span = local_rows // 2
    n_keys = shards * kc
    tk = math.gcd(n_keys, 256)
    rc = heads * span
    dims = (heads, span, hd, shards, kc, tk, rc)
    blocks = span // kc
    ctx = lax.axis_index("ctx")
    head = lax.axis_index("head")

    mesh_x = heads // 2
    part = head // blocks
    own = lax.dynamic_slice_in_dim(span_of, 2 * ctx, 2)
    block = jnp.arange(2 * shards, dtype=jnp.int32)
    mine = block % 2 == part
    below = mine[None, :] & (span_of[None, :] < span_of[:, None])
    rank = jnp.sum(below.astype(jnp.int32), axis=1)
    slot = jnp.arange(shards, dtype=jnp.int32)
    here = mine[None, :] & (rank[None, :] == slot[:, None])
    ordered = jnp.sum(jnp.where(here, span_of[None, :], 0), axis=1)
    kpos = (
        ordered[:, None] * span
        + (head % blocks) * kc
        + jnp.arange(kc, dtype=jnp.int32)[None, :]
    ).reshape(n_keys, 1)
    qpos = own[:, None] * span + jnp.tile(jnp.arange(span, dtype=jnp.int32), heads)[None, :]
    before = mine[None, :] & (span_of[None, :] < own[:, None])
    seen = mine[None, :] & (span_of[None, :] <= own[:, None])
    before = jnp.sum(before.astype(jnp.int32), axis=1) * kc
    seen = jnp.sum(seen.astype(jnp.int32), axis=1) * kc
    full = before // tk
    count = (seen + tk - 1) // tk

    near, kv_all = run_pack(shards, query_in, grad_out, key_in, value_in)
    kv_all = exchange(kv_all, "ctx")
    masks, _ = flips(mesh_x)
    for mask in masks:
        near = jnp.concatenate([near, flip_x(near, mesh_x, mask)])
    far = swap_cores(near, mesh_x)

    stat, kvs, q, d, probs = run_stats(dims, rank, full, count, kpos, qpos, near, far, kv_all)
    rows = 2 * heads * span
    stat_all = exchange(jnp.broadcast_to(stat[None, :2], (heads, 2, rows)), "head")
    keep, send, key_parts = run_grads(
        dims, rank, full, count, stat, stat_all, q, d, kvs, probs
    )
    key_parts = exchange(key_parts, "ctx")

    row_sum = keep.astype(F32) + swap_cores(send, mesh_x).astype(F32)
    for mask in reversed(masks):
        half = row_sum.shape[0] // 2
        moved = flip_x(row_sum[half:].astype(BF16), mesh_x, mask)
        row_sum = row_sum[:half] + moved.astype(F32)
    row_sum = row_sum[0].astype(BF16)
    key_sum = jnp.sum(key_parts.astype(F32), axis=0).astype(BF16)
    width = heads * hd
    return (row_sum[:, :width], row_sum[:, width:], key_sum[:, :hd], key_sum[:, hd:])


def solution(mesh):
    return jax.shard_map(
        local,
        mesh=mesh,
        in_specs=(
            P("ctx", "head"),
            P(("ctx", "head"), None),
            P(("ctx", "head"), None),
            P("ctx", "head"),
            P(),
        ),
        out_specs=(P(("ctx", "head"), None),) * 4,
        check_vma=False,
    )
```
